512 devices in a mesh: dp: 32 (over z_lo, x), sp: 16 (over y, z_hi, core).
Axes of the slice: x: 4, y: 4, z: 16 (z_hi: 2, z_lo: 8; z = z_hi * 8 + z_lo), core: 2. Of those that a mesh axis runs over, the one named last changes fastest.
Arguments:
- query: bfloat16 [4096, 12288], P(('dp', 'sp')), parts along dimension 0, may hold values from -24 to 24
- grad_out: bfloat16 [4096, 8192], P(('dp', 'sp')), parts along dimension 0, may hold values from -6 to 6
- latent: bfloat16 [65536, 512], P(('dp', 'sp')), parts along dimension 0, may hold values from -6 to 6
- rope_key: bfloat16 [65536, 64], P(('dp', 'sp')), parts along dimension 0, may hold values from -6 to 6
- w_key: bfloat16 [512, 8192], P(None, 'sp'), may hold values from -0.5 to 0.5
- w_value: bfloat16 [512, 8192], P(None, 'sp'), may hold values from -0.5 to 0.5
- offset: int32 [32], P('dp'), parts along dimension 0, may hold values from 0 to 1920
Outputs:
- d_query: bfloat16 [4096, 12288], P(('dp', 'sp')), parts along dimension 0
- d_latent: bfloat16 [65536, 512], P(('dp', 'sp')), parts along dimension 0
- d_rope_key: bfloat16 [65536, 64], P(('dp', 'sp')), parts along dimension 0
The draws below stay inside these ranges and needn't reach their ends.
There are 32 independent parts, one for each index of `dp`. The reference program is written for one: setup_inputs(seed, part) draws one part's arguments, and reference() takes and returns one part's arrays. A program takes and returns all parts, laid end to end along the dimension named above; an argument that names none is the same for every part. Nothing has to cross between parts.
All inputs are finite; a program needn't handle non-finite values.
Results may differ from the reference program's by a relative error of at most 0.023.
Values may be sent and summed in bfloat16 or wider, within the bound.
No kernel may reach another device: no remote copies, remote signals or barrier semaphores. Data moves between devices by JAX's collectives and lax.ppermute only.
A program may use at most 64 MiB of HBM per device.

```python
import jax
import jax.numpy as jnp
from jax import lax

HEAD_DEV = 4
NOPE = 128
ROPE = 64
VDIM = 128
LATENT = 512
HEADS = 64
QUERIES = 128
KEYS = 2048
N_SP = 16


def draw_query(key, part):
    key = jax.random.fold_in(key, 11)
    width = NOPE + ROPE
    base = jnp.clip(jax.random.normal(key, (QUERIES, HEADS, width), jnp.float32), -6.0, 6.0)
    return base.reshape(QUERIES, HEADS * width).astype(jnp.bfloat16)


def draw_rope_key(key, part):
    key = jax.random.fold_in(key, 13)
    base = jnp.clip(jax.random.normal(key, (KEYS, ROPE), jnp.float32), -6.0, 6.0)
    return base.astype(jnp.bfloat16)


def block_levels(rng, dims, split, low, largest):
    loudness, own = 1.0, jax.random.fold_in(rng, 6)
    for position, shards_of in split:
        draws = jnp.exp(jax.random.uniform(jax.random.fold_in(own, position), (shards_of,), jnp.float32, low / len(split), largest / len(split)))
        loudness = loudness * jnp.repeat(draws, dims[position] // shards_of).reshape([-1 if axis == position else 1 for axis in range(len(dims))])
    return loudness


def gaussian(own_key, extent, scale, most, shards=(), kind=jnp.bfloat16):
    values = jax.random.normal(own_key, extent, jnp.float32) * scale
    if len(shards) > 0:
        values = block_levels(own_key, extent, shards, -0.22, 0.18) * values
    return jnp.clip(values, min=-most, max=most).astype(kind)


def setup_inputs(seed: int = 0, part: int = 0) -> dict:
    seeds = jax.random.split(jax.random.key(seed), 8)
    own_keys = jax.random.split(jax.random.fold_in(seeds[7], part), 8)
    query = draw_query(jax.random.fold_in(jax.random.fold_in(seeds[7], part), 71), part)
    grad_out = gaussian(own_keys[1], (QUERIES, HEADS * VDIM), 1.0, 6.0, ((0, 16),))
    latent = gaussian(own_keys[2], (KEYS, LATENT), 1.0, 6.0, ((0, 16),))
    rope_key = draw_rope_key(jax.random.fold_in(jax.random.fold_in(seeds[7], part), 71), part)
    w_key = gaussian(seeds[4], (LATENT, HEADS * NOPE), NOPE ** -0.5, 0.5, ((1, 16),))
    w_value = gaussian(seeds[5], (LATENT, HEADS * VDIM), VDIM ** -0.5, 0.5, ((1, 16),))
    offset = jax.random.randint(own_keys[6], (1,), 0, KEYS - QUERIES + 1).astype(jnp.int32)
    return dict(query=query, grad_out=grad_out, latent=latent, rope_key=rope_key, w_key=w_key, w_value=w_value, offset=offset)


def rounded(value):
    return lax.optimization_barrier(value.astype(jnp.bfloat16)).astype(jnp.float32)


def reference(query, grad_out, latent, rope_key, w_key, w_value, offset):
    width = NOPE + ROPE
    scale = width ** -0.5
    query3 = query.astype(jnp.float32).reshape(QUERIES, HEADS, width)
    key_proj = w_key.astype(jnp.float32).reshape(LATENT, HEADS, NOPE)
    value_proj = w_value.astype(jnp.float32).reshape(LATENT, HEADS, VDIM)
    grads3 = grad_out.astype(jnp.float32).reshape(QUERIES, HEADS, VDIM)
    q_plain = query3[:, :, :NOPE]
    q_rot = query3[:, :, NOPE:]
    q_lat = rounded(jnp.einsum('qhn,lhn->hql', q_plain, key_proj))
    d_olat = rounded(jnp.einsum('qhv,lhv->hql', grads3, value_proj))
    lat = latent.astype(jnp.float32)
    rot_key = rope_key.astype(jnp.float32)
    scores = (jnp.einsum('hql,kl->hqk', q_lat, lat) + jnp.einsum('qhr,kr->hqk', q_rot, rot_key)) * scale
    q_pos = offset[0] + jnp.arange(QUERIES, dtype=jnp.int32)
    k_pos = jnp.arange(KEYS, dtype=jnp.int32)
    visible = (k_pos[None, :] <= q_pos[:, None])[None]
    top = jnp.max(jnp.where(visible, scores, -1e30), axis=2, keepdims=True)
    expo = jnp.where(visible, jnp.exp(scores - top), 0.0)
    probs = expo / jnp.sum(expo, axis=2, keepdims=True)
    dprob = jnp.einsum('hql,kl->hqk', d_olat, lat)
    delta = jnp.sum(probs * dprob, axis=2, keepdims=True)
    dscore = rounded(probs * (dprob - delta) * scale)
    probs_low = rounded(probs)
    dq_lat = rounded(jnp.einsum('hqk,kl->hql', dscore, lat))
    dq_rot = jnp.einsum('hqk,kr->qhr', dscore, rot_key).astype(jnp.bfloat16)
    dq_plain = jnp.einsum('hql,lhn->qhn', dq_lat, key_proj).astype(jnp.bfloat16)
    d_query = jnp.concatenate([dq_plain, dq_rot], axis=2).reshape(QUERIES, HEADS * width)
    ds_group = dscore.reshape(N_SP, HEAD_DEV, QUERIES, KEYS)
    pr_group = probs_low.reshape(N_SP, HEAD_DEV, QUERIES, KEYS)
    lat_part = jnp.einsum('ghqk,ghql->gkl', ds_group, q_lat.reshape(N_SP, HEAD_DEV, QUERIES, LATENT))
    lat_part = lat_part + jnp.einsum('ghqk,ghql->gkl', pr_group, d_olat.reshape(N_SP, HEAD_DEV, QUERIES, LATENT))
    rot_part = jnp.einsum('ghqk,qghr->gkr', ds_group, q_rot.reshape(QUERIES, N_SP, HEAD_DEV, ROPE))
    d_latent = jnp.sum(rounded(lat_part), axis=0).astype(jnp.bfloat16)
    d_rope_key = jnp.sum(rounded(rot_part), axis=0).astype(jnp.bfloat16)
    return d_query, d_latent, d_rope_key
```

```python
import jax
import jax.numpy as jnp
from jax import lax
from jax.experimental import pallas as pl
from jax.experimental.pallas import tpu as pltpu
from jax.sharding import Mesh, PartitionSpec as P

NOPE = 128
ROPE = 64
VDIM = 128
LATENT = 512
WIDTH = NOPE + ROPE
KEYED = LATENT + ROPE
N_Y, N_Z, N_C = 4, 2, 2
SWAP = [(0, 1), (1, 0)]


def dot(left, right, left_dim, right_dim):
    return lax.dot_general(
        left,
        right,
        (((left_dim,), (right_dim,)), ((), ())),
        preferred_element_type=jnp.float32,
    )


def attention_kernel(
    bound_ref,
    qg_ref,
    wk_ref,
    wv_ref,
    k00_ref,
    k01_ref,
    k10_ref,
    k11_ref,
    d00_ref,
    d01_ref,
    d10_ref,
    d11_ref,
    dq_ref,
    q_cat,
    o_lat,
    rel,
    expo,
    dprob,
):
    scale = WIDTH ** (-0.5)
    count = qg_ref.shape[0]
    heads = wk_ref.shape[1] // NOPE
    stacked = heads * count
    block = k00_ref.shape[0] // N_Y
    keys = (k00_ref, k01_ref, k10_ref, k11_ref)
    d_keys = (d00_ref, d01_ref, d10_ref, d11_ref)

    rel[...] = lax.broadcasted_iota(jnp.int32, rel.shape, 0) - lax.rem(
        lax.broadcasted_iota(jnp.int32, rel.shape, 1), count
    )
    for h in range(heads):
        rows = slice(h * count, (h + 1) * count)
        cols = slice(h * NOPE, (h + 1) * NOPE)
        plain = qg_ref[:, h * WIDTH : h * WIDTH + NOPE]
        grad = qg_ref[:, heads * WIDTH + h * VDIM : heads * WIDTH + (h + 1) * VDIM]
        q_cat[rows, :LATENT] = dot(plain, wk_ref[:, cols], 1, 1).astype(jnp.bfloat16)
        q_cat[rows, LATENT:] = qg_ref[:, h * WIDTH + NOPE : (h + 1) * WIDTH]
        o_lat[rows, :] = dot(grad, wv_ref[:, cols], 1, 1).astype(jnp.bfloat16)

    top = jnp.full((1, stacked), -1e30, jnp.float32)
    total = jnp.zeros((1, stacked), jnp.float32)
    delta = jnp.zeros((1, stacked), jnp.float32)
    tops = []
    for n, key_ref in enumerate(keys):
        base = n * N_Y * block
        scores = dot(key_ref[...], q_cat[...], 1, 1) * scale
        dp = dot(key_ref[:, :LATENT], o_lat[...], 1, 1)
        dprob[base : base + N_Y * block, :] = dp
        visible = [rel[...] <= bound_ref[n * N_Y + j] for j in range(N_Y)]
        parts = [
            jnp.where(visible[j], scores[j * block : (j + 1) * block], -1e30)
            for j in range(N_Y)
        ]
        new_top = top
        for part in parts:
            new_top = jnp.maximum(new_top, jnp.max(part, axis=0, keepdims=True))
        keep = jnp.exp(top - new_top)
        total = total * keep
        delta = delta * keep
        for j, part in enumerate(parts):
            e = jnp.where(visible[j], jnp.exp(part - new_top), 0.0)
            expo[base + j * block : base + (j + 1) * block, :] = e
            total += jnp.sum(e, axis=0, keepdims=True)
            delta += jnp.sum(e * dp[j * block : (j + 1) * block], axis=0, keepdims=True)
        top = new_top
        tops.append(new_top)

    inverse = 1.0 / total
    delta = delta * inverse
    dq_lat = jnp.zeros((stacked, KEYED), jnp.float32)
    for n, (key_ref, d_ref) in enumerate(zip(keys, d_keys)):
        base = n * N_Y * block
        span = slice(base, base + N_Y * block)
        probs = expo[span, :] * (jnp.exp(tops[n] - top) * inverse)
        dscore = (probs * (dprob[span, :] - delta) * scale).astype(jnp.bfloat16)
        probs_low = probs.astype(jnp.bfloat16)
        d_key = dot(dscore, q_cat[...], 1, 0)
        d_ref[:, :LATENT] = (
            d_key[:, :LATENT] + dot(probs_low, o_lat[...], 1, 0)
        ).astype(jnp.bfloat16)
        d_ref[:, LATENT:] = d_key[:, LATENT:].astype(jnp.bfloat16)
        dq_lat += dot(dscore, key_ref[...], 0, 0)
    dq_low = dq_lat.astype(jnp.bfloat16)
    for h in range(heads):
        rows = slice(h * count, (h + 1) * count)
        cols = slice(h * NOPE, (h + 1) * NOPE)
        dq_ref[:, h * WIDTH : h * WIDTH + NOPE] = dot(
            dq_low[rows, :LATENT], wk_ref[:, cols], 1, 0
        ).astype(jnp.bfloat16)
        dq_ref[:, h * WIDTH + NOPE : (h + 1) * WIDTH] = dq_low[rows, LATENT:]


def attention(bounds, qg, w_key, w_value, keys):
    count = qg.shape[0]
    heads = w_key.shape[1] // NOPE
    stacked = heads * count
    chunk = keys[0].shape[0]
    total = len(keys) * chunk
    vmem = pl.BlockSpec(memory_space=pltpu.VMEM)
    return pl.pallas_call(
        attention_kernel,
        out_shape=[jax.ShapeDtypeStruct((chunk, KEYED), jnp.bfloat16) for _ in keys]
        + [jax.ShapeDtypeStruct((count, heads * WIDTH), jnp.bfloat16)],
        in_specs=[pl.BlockSpec(memory_space=pltpu.SMEM)] + [vmem] * (3 + len(keys)),
        out_specs=[vmem] * (len(keys) + 1),
        scratch_shapes=[
            pltpu.VMEM((stacked, KEYED), jnp.bfloat16),
            pltpu.VMEM((stacked, LATENT), jnp.bfloat16),
            pltpu.VMEM((chunk // N_Y, stacked), jnp.int32),
            pltpu.VMEM((total, stacked), jnp.float32),
            pltpu.VMEM((total, stacked), jnp.float32),
        ],
        compiler_params=pltpu.CompilerParams(vmem_limit_bytes=48 * 2**20),
        cost_estimate=pl.CostEstimate(
            flops=2 * total * stacked * (3 * KEYED + 2 * LATENT),
            bytes_accessed=4 * total * KEYED,
            transcendentals=total * stacked,
        ),
    )(bounds, qg, w_key, w_value, *keys)


def shift(block, by):
    return lax.ppermute(block, "y", [(i, (i + by) % N_Y) for i in range(N_Y)])


def gather_y(block):
    return jnp.concatenate([block] + [shift(block, s) for s in range(1, N_Y)], axis=0)


def scatter_y(mine, other):
    block = mine.shape[0] // N_Y
    parts = []
    for s in range(N_Y):
        span = slice(s * block, (s + 1) * block)
        parts.append(
            (mine[span].astype(jnp.float32) + other[span].astype(jnp.float32)).astype(
                jnp.bfloat16
            )
        )
    summed = parts[0].astype(jnp.float32)
    for s in range(1, N_Y):
        summed += shift(parts[s], -s).astype(jnp.float32)
    return summed


def on_device(query, grad_out, latent, rope_key, w_key, w_value, offset):
    rows = query.shape[0]
    n_sp = N_Y * N_Z * N_C
    block = latent.shape[0]
    keyed = jnp.concatenate([latent, rope_key], axis=1)
    far = lax.ppermute(keyed, "z", SWAP)
    qg = jnp.concatenate(
        [query.reshape(rows, n_sp, -1), grad_out.reshape(rows, n_sp, -1)], axis=2
    ).reshape(rows, -1)
    qg = lax.all_to_all(qg, ("y", "z", "c"), split_axis=1, concat_axis=0, tiled=True)
    near_mine = gather_y(keyed)
    near_other = lax.ppermute(near_mine, "c", SWAP)
    far_mine = gather_y(far)
    far_other = lax.ppermute(far_mine, "c", SWAP)
    y, z, c = lax.axis_index("y"), lax.axis_index("z"), lax.axis_index("c")
    starts = []
    for dz, dc in ((1, 1), (1, 0), (0, 1), (0, 0)):
        for s in range(N_Y):
            slot = (lax.rem(y - s + N_Y, N_Y) * N_Z + (z ^ dz)) * N_C + (c ^ dc)
            starts.append(slot * block)
    bounds = offset[0] - jnp.stack(starts).astype(jnp.int32)
    d_far_other, d_far_mine, d_near_other, d_near_mine, dq = attention(
        bounds, qg, w_key, w_value, (far_other, far_mine, near_other, near_mine)
    )
    far_got = lax.ppermute(d_far_other, "c", SWAP)
    near_got = lax.ppermute(d_near_other, "c", SWAP)
    d_query = lax.all_to_all(dq, ("y", "z", "c"), split_axis=0, concat_axis=1, tiled=True)
    far_sum = scatter_y(d_far_mine, far_got).astype(jnp.bfloat16)
    back = lax.ppermute(far_sum, "z", SWAP)
    near_sum = scatter_y(d_near_mine, near_got)
    summed = near_sum + back.astype(jnp.float32)
    d_latent = summed[:, :LATENT].astype(jnp.bfloat16)
    d_rope_key = summed[:, LATENT:].astype(jnp.bfloat16)
    return (d_query, d_latent, d_rope_key)


def solution(mesh):
    parts = mesh.devices.shape[0]
    split = Mesh(
        mesh.devices.reshape(parts, N_Y, N_Z, N_C), ("dp", "y", "z", "c")
    )
    rows = P(("dp", "y", "z", "c"), None)
    columns = P(None, ("y", "z", "c"))
    return jax.shard_map(
        on_device,
        mesh=split,
        in_specs=(rows, rows, rows, rows, columns, columns, P("dp")),
        out_specs=(rows, rows, rows),
        check_vma=False,
    )
```

```python
import jax
import jax.numpy as jnp
from jax import lax
from jax.experimental import pallas as pl
from jax.experimental.pallas import tpu as pltpu
from jax.sharding import Mesh, PartitionSpec as P

NOPE = 128
ROPE = 64
VDIM = 128
LATENT = 512
LANES = 128
WIDTH = NOPE + ROPE
KEYED = LATENT + ROPE
N_Y, N_Z, N_C = 4, 2, 2
SWAP = [(0, 1), (1, 0)]
BF16 = jnp.bfloat16
F32 = jnp.float32


def dot(left, right, left_dim, right_dim):
    return lax.dot_general(
        left,
        right,
        (((left_dim,), (right_dim,)), ((), ())),
        preferred_element_type=F32,
    )


def attention_kernel(
    bound_ref,
    row_ref,
    slot_ref,
    qg_hbm,
    wk_hbm,
    wv_hbm,
    far_other_hbm,
    far_mine_hbm,
    near_other_hbm,
    near_mine_hbm,
    d_far_other_hbm,
    d_far_mine_hbm,
    d_near_other_hbm,
    d_near_mine_hbm,
    qg_ref,
    wk_ref,
    wv_ref,
    packed,
    keyed,
    d_near,
    d_far,
    dq_ref,
    q_cat,
    o_lat,
    rel,
    expo,
    dprob,
    in_sem,
    out_sem,
):
    scale = WIDTH ** (-0.5)
    count = qg_ref.shape[0]
    heads = wk_ref.shape[1] // NOPE
    stacked = heads * count
    block = rel.shape[0]
    chunk = N_Y * block
    n_chunks = N_Z * N_C
    folds = LATENT // LANES
    tall = ROPE // folds
    slab = folds * block + ROPE
    keys_hbm = (far_other_hbm, far_mine_hbm, near_other_hbm, near_mine_hbm)

    loads = [
        pltpu.make_async_copy(qg_hbm, qg_ref, in_sem.at[0]),
        pltpu.make_async_copy(wk_hbm, wk_ref, in_sem.at[1]),
        pltpu.make_async_copy(wv_hbm, wv_ref, in_sem.at[2]),
    ] + [
        pltpu.make_async_copy(ref, packed.at[n], in_sem.at[3 + n])
        for n, ref in enumerate(keys_hbm)
    ]
    for load in loads:
        load.start()

    rel[...] = lax.broadcasted_iota(jnp.int32, rel.shape, 0) - lax.rem(
        lax.broadcasted_iota(jnp.int32, rel.shape, 1), count
    )
    for load in loads[:3]:
        load.wait()
    for h in range(heads):
        rows = slice(h * count, (h + 1) * count)
        cols = slice(h * NOPE, (h + 1) * NOPE)
        plain = qg_ref[:, h * WIDTH : h * WIDTH + NOPE]
        grad = qg_ref[:, heads * WIDTH + h * VDIM : heads * WIDTH + (h + 1) * VDIM]
        q_cat[rows, :LATENT] = dot(plain, wk_ref[:, cols], 1, 1).astype(BF16)
        q_cat[rows, LATENT:] = qg_ref[:, h * WIDTH + NOPE : (h + 1) * WIDTH]
        o_lat[rows, :] = dot(grad, wv_ref[:, cols], 1, 1).astype(BF16)

    top = jnp.full((1, stacked), -1e30, F32)
    total = jnp.zeros((1, stacked), F32)
    delta = jnp.zeros((1, stacked), F32)
    tops = []
    for n in range(n_chunks):
        loads[3 + n].wait()
        base = n * chunk
        for j in range(N_Y):
            span = slice(base + j * block, base + (j + 1) * block)
            keyed[span, :LATENT] = packed[n, j, :block, :]
            rot = jnp.concatenate(
                [packed[n, j, block:, a * LANES : (a + 1) * LANES] for a in range(folds)],
                axis=0,
            )
            keyed[span, LATENT:] = jnp.transpose(rot)
        span = slice(base, base + chunk)
        scores = dot(keyed[span, :], q_cat[...], 1, 1) * scale
        dp = dot(keyed[span, :LATENT], o_lat[...], 1, 1)
        dprob[span, :] = dp
        visible = [rel[...] <= bound_ref[n * N_Y + j] for j in range(N_Y)]
        parts = [
            jnp.where(visible[j], scores[j * block : (j + 1) * block], -1e30)
            for j in range(N_Y)
        ]
        new_top = top
        for part in parts:
            new_top = jnp.maximum(new_top, jnp.max(part, axis=0, keepdims=True))
        keep = jnp.exp(top - new_top)
        total = total * keep
        delta = delta * keep
        for j, part in enumerate(parts):
            e = jnp.where(visible[j], jnp.exp(part - new_top), 0.0)
            expo[base + j * block : base + (j + 1) * block, :] = e
            total += jnp.sum(e, axis=0, keepdims=True)
            delta += jnp.sum(e * dp[j * block : (j + 1) * block], axis=0, keepdims=True)
        top = new_top
        tops.append(new_top)

    inverse = 1.0 / total
    delta = delta * inverse
    dq_lat = jnp.zeros((stacked, KEYED), F32)
    stores = []
    for n in (2, 3, 0, 1):
        span = slice(n * chunk, (n + 1) * chunk)
        probs = expo[span, :] * (jnp.exp(tops[n] - top) * inverse)
        dscore = (probs * (dprob[span, :] - delta) * scale).astype(BF16)
        probs_low = probs.astype(BF16)
        d_key = dot(dscore, q_cat[...], 1, 0)
        d_lat = (d_key[:, :LATENT] + dot(probs_low, o_lat[...], 1, 0)).astype(BF16)
        d_rot = d_key[:, LATENT:].astype(BF16)
        for j in range(N_Y):
            rows = slice(j * block, (j + 1) * block)
            place = d_far.at[n, slot_ref[j]] if n < 2 else d_near.at[n - 2, slot_ref[j]]
            for a in range(folds):
                place[a * block : (a + 1) * block, :] = d_lat[
                    rows, a * LANES : (a + 1) * LANES
                ]
            place[folds * block : slab, :] = jnp.transpose(d_rot[rows])
        if n >= 2:
            store = pltpu.make_async_copy(
                d_near.at[n - 2],
                (d_near_other_hbm, d_near_mine_hbm)[n - 2],
                out_sem.at[n],
            )
            store.start()
            stores.append(store)
        dq_lat += dot(dscore, keyed[span, :], 0, 0)
    dq_low = dq_lat.astype(BF16)
    for h in range(heads):
        rows = slice(h * count, (h + 1) * count)
        cols = slice(h * NOPE, (h + 1) * NOPE)
        dq_ref[:, h * WIDTH : h * WIDTH + NOPE] = dot(
            dq_low[rows, :LATENT], wk_ref[:, cols], 1, 0
        )
        dq_ref[:, h * WIDTH + NOPE : (h + 1) * WIDTH] = dq_lat[rows, LATENT:]
    few = count // (N_Y * N_Z * N_C)
    for n in range(N_C):
        for j in range(N_Y):
            pieces = []
            for dz in range(N_Z):
                start = pl.multiple_of(row_ref[(n * N_Y + j) * N_Z + dz], few)
                for a in range(heads * WIDTH // LANES):
                    pieces.append(dq_ref[pl.ds(start, few), a * LANES : (a + 1) * LANES])
            d_far[n, j, slab:, :] = jnp.concatenate(pieces, axis=0).astype(BF16)
        store = pltpu.make_async_copy(
            d_far.at[n], (d_far_other_hbm, d_far_mine_hbm)[n], out_sem.at[n]
        )
        store.start()
        stores.append(store)
    for store in stores:
        store.wait()


def attention(bounds, starts, slots, qg, w_key, w_value, far_other, far_mine, near_other, near_mine):
    count = qg.shape[0]
    heads = w_key.shape[1] // NOPE
    stacked = heads * count
    tall = near_mine.shape[1]
    block = tall * LATENT // KEYED
    n_chunks = N_Z * N_C
    total = n_chunks * N_Y * block
    slab = block * KEYED // LANES
    extra = N_Z * (count // (N_Y * N_Z * N_C)) * heads * WIDTH // LANES
    hbm = pl.BlockSpec(memory_space=pl.ANY)
    smem = pl.BlockSpec(memory_space=pltpu.SMEM)
    return pl.pallas_call(
        attention_kernel,
        out_shape=[
            jax.ShapeDtypeStruct((N_Y, slab + extra, LANES), BF16),
            jax.ShapeDtypeStruct((N_Y, slab + extra, LANES), BF16),
            jax.ShapeDtypeStruct((N_Y, slab, LANES), BF16),
            jax.ShapeDtypeStruct((N_Y, slab, LANES), BF16),
        ],
        in_specs=[smem] * 3 + [hbm] * 7,
        out_specs=[hbm] * 4,
        scratch_shapes=[
            pltpu.VMEM(qg.shape, BF16),
            pltpu.VMEM(w_key.shape, BF16),
            pltpu.VMEM(w_value.shape, BF16),
            pltpu.VMEM((n_chunks, N_Y, tall, LATENT), BF16),
            pltpu.VMEM((total, KEYED), BF16),
            pltpu.VMEM((N_C, N_Y, slab, LANES), BF16),
            pltpu.VMEM((N_C, N_Y, slab + extra, LANES), BF16),
            pltpu.VMEM((count, heads * WIDTH), F32),
            pltpu.VMEM((stacked, KEYED), BF16),
            pltpu.VMEM((stacked, LATENT), BF16),
            pltpu.VMEM((block, stacked), jnp.int32),
            pltpu.VMEM((total, stacked), F32),
            pltpu.VMEM((total, stacked), F32),
            pltpu.SemaphoreType.DMA((3 + n_chunks,)),
            pltpu.SemaphoreType.DMA((n_chunks,)),
        ],
        compiler_params=pltpu.CompilerParams(vmem_limit_bytes=56 * 2**20),
        cost_estimate=pl.CostEstimate(
            flops=2 * total * stacked * (3 * KEYED + 2 * LATENT),
            bytes_accessed=4 * total * KEYED,
            transcendentals=total * stacked,
        ),
    )(bounds, starts, slots, qg, w_key, w_value, far_other, far_mine, near_other, near_mine)


def shift(block, by):
    return lax.ppermute(block, "y", [(i, (i + by) % N_Y) for i in range(N_Y)])


def on_device(query, grad_out, latent, rope_key, w_key, w_value, offset):
    few = query.shape[0]
    n_sp = N_Y * N_Z * N_C
    block = latent.shape[0]
    folds = LATENT // LANES
    y, z, c = lax.axis_index("y"), lax.axis_index("z"), lax.axis_index("c")
    turned = rope_key.T.reshape(folds, ROPE // folds, block)
    pack = jnp.concatenate(
        [latent, jnp.transpose(turned, (1, 0, 2)).reshape(-1, LATENT)], axis=0
    )
    far = lax.ppermute(pack, "z", SWAP)
    qg = jnp.concatenate(
        [query.reshape(few, n_sp, -1), grad_out.reshape(few, n_sp, -1)], axis=2
    ).reshape(few, -1)
    qg, pack = lax.optimization_barrier((qg, pack))
    near_mine = [pack] + [shift(pack, s) for s in range(1, N_Y)]
    qg, near_mine[1] = lax.optimization_barrier((qg, near_mine[1]))
    near_mine = jnp.stack(near_mine)
    qg = lax.all_to_all(qg, ("y", "z", "c"), split_axis=1, concat_axis=0, tiled=True)
    near_other = lax.ppermute(near_mine, "c", SWAP)
    far_mine = jnp.stack([far] + [shift(far, s) for s in range(1, N_Y)])
    far_other = lax.ppermute(far_mine, "c", SWAP)

    steps = jnp.arange(N_Y, dtype=jnp.int32)

    def owner(y_of, z_of, c_of):
        return ((y_of * N_Z + z_of) * N_C + c_of).astype(jnp.int32)

    shifted = lax.rem(y - steps + N_Y, N_Y)
    owners = [owner(shifted, z ^ dz, c ^ dc) for dz in (1, 0) for dc in (1, 0)]
    bounds = offset[0] - jnp.concatenate(owners) * block
    starts = jnp.stack(
        [
            owner(steps[:, None], z ^ jnp.array([[1, 0]]), c ^ dc).reshape(-1)
            for dc in (1, 0)
        ]
    ).reshape(-1)
    d_other, d_mine, d_near_other, d_near_mine = attention(
        bounds,
        starts * few,
        shifted.astype(jnp.int32),
        qg,
        w_key,
        w_value,
        far_other,
        far_mine,
        near_other,
        near_mine,
    )
    slab = d_near_mine.shape[1]
    got = lax.ppermute(d_other, "c", SWAP)
    summed = d_mine[:, :slab].astype(F32) + got[:, :slab].astype(F32)
    sent = jnp.concatenate([summed.astype(BF16), d_mine[:, slab:], got[:, slab:]], axis=1)
    sent, d_near_other = lax.optimization_barrier((sent, d_near_other))
    near_got = lax.ppermute(d_near_other, "c", SWAP)
    near_half = (d_near_mine.astype(F32) + near_got.astype(F32)).astype(BF16)
    slots = lax.all_to_all(sent, "y", split_axis=0, concat_axis=0, tiled=True)
    far_sum = jnp.sum(slots[:, :slab].astype(F32), axis=0).astype(BF16)
    piece = (d_mine.shape[1] - slab) // N_Z
    parts = slots[:, slab:].reshape(N_Y, N_C, N_Z, piece, LANES)
    leaving = jnp.concatenate([far_sum, parts[:, :, 0].reshape(-1, LANES)], axis=0)
    back = lax.ppermute(leaving, "z", SWAP)
    _, near_half = lax.optimization_barrier((leaving, near_half))
    near_sum = lax.all_to_all(near_half, "y", split_axis=0, concat_axis=0, tiled=True)
    near_sum = jnp.sum(near_sum.astype(F32), axis=0)
    summed = (near_sum + back[:slab].astype(F32)).astype(BF16)
    d_latent = jnp.transpose(
        summed[: folds * block].reshape(folds, block, LANES), (1, 0, 2)
    ).reshape(block, LATENT)
    d_rope_key = summed[folds * block :].T
    both = jnp.stack(
        [parts[:, :, 1], back[slab:].reshape(N_Y, N_C, piece, LANES)]
    ).reshape(N_Z, N_Y, N_C, -1, few, LANES)
    both = jnp.where(z == 1, both[::-1], both)
    both = jnp.where(c == 1, both[:, :, ::-1], both)
    d_query = jnp.transpose(both, (4, 1, 0, 2, 3, 5)).reshape(few, -1)
    return (d_query, d_latent, d_rope_key)


def solution(mesh):
    parts = mesh.devices.shape[0]
    split = Mesh(mesh.devices.reshape(parts, N_Y, N_Z, N_C), ("dp", "y", "z", "c"))
    rows = P(("dp", "y", "z", "c"), None)
    columns = P(None, ("y", "z", "c"))
    return jax.shard_map(
        on_device,
        mesh=split,
        in_specs=(rows, rows, rows, rows, columns, columns, P("dp")),
        out_specs=(rows, rows, rows),
        check_vma=False,
    )
```

```python
import math

import jax
import jax.numpy as jnp
from jax import lax
from jax.experimental import pallas as pl
from jax.experimental.pallas import tpu as pltpu
from jax.sharding import Mesh, PartitionSpec as P

NOPE = 128
ROPE = 64
VDIM = 128
LATENT = 512
LANES = 128
WIDTH = NOPE + ROPE
KEYED = LATENT + ROPE
N_Y, N_Z, N_C = 4, 2, 2
SWAP = [(0, 1), (1, 0)]
BF16 = jnp.bfloat16
F32 = jnp.float32
LOWEST = -1e29
HIDDEN = -1e30
EXPONENT = math.log2(math.e) * WIDTH ** (-0.5)
ORDER_FLOPS = 20_000_000_000
NEAR_FLOPS = 6_000_000_000


def dot(left, right, left_dim, right_dim):
    return lax.dot_general(
        left,
        right,
        (((left_dim,), (right_dim,)), ((), ())),
        preferred_element_type=F32,
    )


def unpack_keys(packed, keyed, base):
    block = packed.shape[1] * LATENT // KEYED
    folds = LATENT // LANES
    for j in range(N_Y):
        span = slice(base + j * block, base + (j + 1) * block)
        keyed[span, :LATENT] = packed[j, :block, :]
        rot = jnp.concatenate(
            [packed[j, block:, a * LANES : (a + 1) * LANES] for a in range(folds)], axis=0
        )
        keyed[span, LATENT:] = jnp.transpose(rot)


def forward_chunk(n, base, carry, bound_ref, rel, keyed, q_cat, o_lat, expo, dprob):
    top, total, delta = carry
    block = rel.shape[0]
    span = slice(base, base + N_Y * block)
    scores = dot(keyed[span, :], q_cat[...], 1, 1)
    dp = dot(keyed[span, :LATENT], o_lat[...], 1, 1)
    dprob[span, :] = dp
    visible = [rel[...] <= bound_ref[n * N_Y + j] for j in range(N_Y)]
    parts = [
        jnp.where(visible[j], scores[j * block : (j + 1) * block], HIDDEN)
        for j in range(N_Y)
    ]
    new_top = top
    for part in parts:
        new_top = jnp.maximum(new_top, jnp.max(part, axis=0, keepdims=True))
    keep = jnp.exp2((top - new_top) * EXPONENT)
    total = total * keep
    delta = delta * keep
    for j, part in enumerate(parts):
        e = jnp.exp2((part - new_top) * EXPONENT)
        expo[base + j * block : base + (j + 1) * block, :] = e
        total += jnp.sum(e, axis=0, keepdims=True)
        delta += jnp.sum(e * dp[j * block : (j + 1) * block], axis=0, keepdims=True)
    return new_top, total, delta


def set_relative(rel, count):
    rel[...] = lax.broadcasted_iota(jnp.int32, rel.shape, 0) - lax.rem(
        lax.broadcasted_iota(jnp.int32, rel.shape, 1), count
    )


def first_kernel(
    bound_ref,
    qg_hbm,
    wk_hbm,
    wv_hbm,
    keys_hbm,
    q_cat_hbm,
    o_lat_hbm,
    keyed_hbm,
    expo_hbm,
    dprob_hbm,
    stats_ref,
    qg_ref,
    wk_ref,
    wv_ref,
    packed,
    keyed,
    q_cat,
    o_lat,
    rel,
    expo,
    dprob,
    in_sem,
    out_sem,
):
    count = qg_ref.shape[0]
    heads = wk_ref.shape[1] // NOPE
    stacked = heads * count
    chunk = N_Y * rel.shape[0]
    loads = [
        pltpu.make_async_copy(qg_hbm, qg_ref, in_sem.at[0]),
        pltpu.make_async_copy(wk_hbm, wk_ref, in_sem.at[1]),
        pltpu.make_async_copy(wv_hbm, wv_ref, in_sem.at[2]),
        pltpu.make_async_copy(keys_hbm, packed, in_sem.at[3]),
    ]
    for load in loads:
        load.start()
    set_relative(rel, count)
    for load in loads:
        load.wait()
    for h in range(heads):
        rows = slice(h * count, (h + 1) * count)
        cols = slice(h * NOPE, (h + 1) * NOPE)
        plain = qg_ref[:, h * WIDTH : h * WIDTH + NOPE]
        grad = qg_ref[:, heads * WIDTH + h * VDIM : heads * WIDTH + (h + 1) * VDIM]
        q_cat[rows, :LATENT] = dot(plain, wk_ref[:, cols], 1, 1).astype(BF16)
        q_cat[rows, LATENT:] = qg_ref[:, h * WIDTH + NOPE : (h + 1) * WIDTH]
        o_lat[rows, :] = dot(grad, wv_ref[:, cols], 1, 1).astype(BF16)
    carry = (
        jnp.full((1, stacked), LOWEST, F32),
        jnp.zeros((1, stacked), F32),
        jnp.zeros((1, stacked), F32),
    )
    stores = [
        pltpu.make_async_copy(q_cat, q_cat_hbm, out_sem.at[0]),
        pltpu.make_async_copy(o_lat, o_lat_hbm, out_sem.at[1]),
    ]
    for store in stores:
        store.start()
    for n in range(N_Z):
        unpack_keys(packed.at[n], keyed, n * chunk)
        carry = forward_chunk(
            n, n * chunk, carry, bound_ref, rel, keyed, q_cat, o_lat, expo, dprob
        )
        span = pl.ds(n * chunk, chunk)
        for i, (mine, out) in enumerate(
            ((keyed, keyed_hbm), (expo, expo_hbm), (dprob, dprob_hbm))
        ):
            store = pltpu.make_async_copy(
                mine.at[span], out.at[span], out_sem.at[2 + 3 * n + i]
            )
            store.start()
            stores.append(store)
        stats_ref[n : n + 1, :] = carry[0]
    stats_ref[N_Z : N_Z + 1, :] = carry[1]
    stats_ref[N_Z + 1 : N_Z + 2, :] = carry[2]
    for store in stores:
        store.wait()


def second_kernel(
    bound_ref,
    row_ref,
    slot_ref,
    stats_ref,
    q_cat_hbm,
    o_lat_hbm,
    wk_hbm,
    keys_hbm,
    keyed_hbm,
    expo_hbm,
    dprob_hbm,
    d_far_other_hbm,
    d_far_mine_hbm,
    d_near_other_hbm,
    d_near_mine_hbm,
    wk_ref,
    packed,
    keyed,
    d_near,
    d_far,
    dq_ref,
    q_cat,
    o_lat,
    rel,
    expo,
    dprob,
    in_sem,
    out_sem,
):
    scale = WIDTH ** (-0.5)
    heads = wk_ref.shape[1] // NOPE
    stacked = q_cat.shape[0]
    count = stacked // heads
    block = rel.shape[0]
    chunk = N_Y * block
    half = N_Z * chunk
    folds = LATENT // LANES
    slab = folds * block + ROPE
    late = pl.ds(half, half)
    loads = [
        pltpu.make_async_copy(keys_hbm, packed, in_sem.at[0]),
        pltpu.make_async_copy(q_cat_hbm, q_cat, in_sem.at[1]),
        pltpu.make_async_copy(o_lat_hbm, o_lat, in_sem.at[2]),
        pltpu.make_async_copy(keyed_hbm, keyed.at[late], in_sem.at[3]),
        pltpu.make_async_copy(expo_hbm, expo.at[late], in_sem.at[4]),
        pltpu.make_async_copy(dprob_hbm, dprob.at[late], in_sem.at[5]),
        pltpu.make_async_copy(wk_hbm, wk_ref, in_sem.at[6]),
    ]
    for load in loads:
        load.start()
    set_relative(rel, count)
    for load in loads[:3]:
        load.wait()
    carry = (
        stats_ref[N_Z - 1 : N_Z, :],
        stats_ref[N_Z : N_Z + 1, :],
        stats_ref[N_Z + 1 : N_Z + 2, :],
    )
    tops = []
    for n in range(N_Z):
        unpack_keys(packed.at[n], keyed, n * chunk)
        carry = forward_chunk(
            n, n * chunk, carry, bound_ref, rel, keyed, q_cat, o_lat, expo, dprob
        )
        tops.append(carry[0])
    tops += [stats_ref[n : n + 1, :] for n in range(N_Z)]
    for load in loads[3:]:
        load.wait()
    top, total, delta = carry
    inverse = 1.0 / total
    delta = delta * inverse
    dq_lat = jnp.zeros((stacked, KEYED), F32)
    stores = []
    for m in (0, 2, 1, 3):
        z_slot, c_slot = m % N_Z, m // N_Z
        span = slice(m * chunk, (m + 1) * chunk)
        probs = expo[span, :] * (jnp.exp2((tops[m] - top) * EXPONENT) * inverse)
        dscore = (probs * (dprob[span, :] - delta) * scale).astype(BF16)
        probs_low = probs.astype(BF16)
        d_key = dot(dscore, q_cat[...], 1, 0)
        d_lat = (d_key[:, :LATENT] + dot(probs_low, o_lat[...], 1, 0)).astype(BF16)
        d_rot = d_key[:, LATENT:].astype(BF16)
        for j in range(N_Y):
            rows = slice(j * block, (j + 1) * block)
            place = (d_far, d_near)[z_slot].at[c_slot, slot_ref[j]]
            for a in range(folds):
                place[a * block : (a + 1) * block, :] = d_lat[
                    rows, a * LANES : (a + 1) * LANES
                ]
            place[folds * block : slab, :] = jnp.transpose(d_rot[rows])
        if z_slot == 0:
            store = pltpu.make_async_copy(
                d_far.at[c_slot],
                (d_far_other_hbm, d_far_mine_hbm)[c_slot],
                out_sem.at[c_slot],
            )
            store.start()
            stores.append(store)
        dq_lat += dot(dscore, keyed[span, :], 0, 0)
    dq_low = dq_lat.astype(BF16)
    for h in range(heads):
        rows = slice(h * count, (h + 1) * count)
        cols = slice(h * NOPE, (h + 1) * NOPE)
        dq_ref[:, h * WIDTH : h * WIDTH + NOPE] = dot(
            dq_low[rows, :LATENT], wk_ref[:, cols], 1, 0
        )
        dq_ref[:, h * WIDTH + NOPE : (h + 1) * WIDTH] = dq_lat[rows, LATENT:]
    few = count // (N_Y * N_Z * N_C)
    for n in range(N_C):
        for j in range(N_Y):
            pieces = []
            for dz in range(N_Z):
                start = pl.multiple_of(row_ref[(n * N_Y + j) * N_Z + dz], few)
                for a in range(heads * WIDTH // LANES):
                    pieces.append(dq_ref[pl.ds(start, few), a * LANES : (a + 1) * LANES])
            d_near[n, j, slab:, :] = jnp.concatenate(pieces, axis=0).astype(BF16)
        store = pltpu.make_async_copy(
            d_near.at[n], (d_near_other_hbm, d_near_mine_hbm)[n], out_sem.at[N_C + n]
        )
        store.start()
        stores.append(store)
    for store in stores:
        store.wait()


def attention(bounds_mine, bounds_other, starts, slots, qg, w_key, w_value, mine, other):
    count = qg.shape[0]
    heads = w_key.shape[1] // NOPE
    stacked = heads * count
    tall = mine.shape[2]
    block = tall * LATENT // KEYED
    half = N_Z * N_Y * block
    slab = block * KEYED // LANES
    extra = N_Z * (count // (N_Y * N_Z * N_C)) * heads * WIDTH // LANES
    near_slab = slab + extra
    hbm = pl.BlockSpec(memory_space=pl.ANY)
    smem = pl.BlockSpec(memory_space=pltpu.SMEM)
    vmem = pl.BlockSpec(memory_space=pltpu.VMEM)
    middle = [
        jax.ShapeDtypeStruct((stacked, KEYED), BF16),
        jax.ShapeDtypeStruct((stacked, LATENT), BF16),
        jax.ShapeDtypeStruct((half, KEYED), BF16),
        jax.ShapeDtypeStruct((half, stacked), F32),
        jax.ShapeDtypeStruct((half, stacked), F32),
        jax.ShapeDtypeStruct((8, stacked), F32),
    ]
    q_cat, o_lat, keyed, expo, dprob, stats = pl.pallas_call(
        first_kernel,
        out_shape=middle,
        in_specs=[smem] + [hbm] * 4,
        out_specs=[hbm] * 5 + [vmem],
        scratch_shapes=[
            pltpu.VMEM(qg.shape, BF16),
            pltpu.VMEM(w_key.shape, BF16),
            pltpu.VMEM(w_value.shape, BF16),
            pltpu.VMEM(mine.shape, BF16),
            pltpu.VMEM((half, KEYED), BF16),
            pltpu.VMEM((stacked, KEYED), BF16),
            pltpu.VMEM((stacked, LATENT), BF16),
            pltpu.VMEM((block, stacked), jnp.int32),
            pltpu.VMEM((half, stacked), F32),
            pltpu.VMEM((half, stacked), F32),
            pltpu.SemaphoreType.DMA((4,)),
            pltpu.SemaphoreType.DMA((2 + 3 * N_Z,)),
        ],
        compiler_params=pltpu.CompilerParams(vmem_limit_bytes=56 * 2**20),
        cost_estimate=pl.CostEstimate(
            flops=ORDER_FLOPS, bytes_accessed=12 * half * stacked, transcendentals=half * stacked
        ),
    )(bounds_mine, qg, w_key, w_value, mine)
    return pl.pallas_call(
        second_kernel,
        out_shape=[jax.ShapeDtypeStruct((N_Y, slab, LANES), BF16)] * N_C
        + [jax.ShapeDtypeStruct((N_Y, near_slab, LANES), BF16)] * N_C,
        in_specs=[smem] * 3 + [vmem] + [hbm] * 7,
        out_specs=[hbm] * 4,
        scratch_shapes=[
            pltpu.VMEM(w_key.shape, BF16),
            pltpu.VMEM(other.shape, BF16),
            pltpu.VMEM((2 * half, KEYED), BF16),
            pltpu.VMEM((N_C, N_Y, near_slab, LANES), BF16),
            pltpu.VMEM((N_C, N_Y, slab, LANES), BF16),
            pltpu.VMEM((count, heads * WIDTH), F32),
            pltpu.VMEM((stacked, KEYED), BF16),
            pltpu.VMEM((stacked, LATENT), BF16),
            pltpu.VMEM((block, stacked), jnp.int32),
            pltpu.VMEM((2 * half, stacked), F32),
            pltpu.VMEM((2 * half, stacked), F32),
            pltpu.SemaphoreType.DMA((7,)),
            pltpu.SemaphoreType.DMA((2 * N_C,)),
        ],
        compiler_params=pltpu.CompilerParams(vmem_limit_bytes=56 * 2**20),
        cost_estimate=pl.CostEstimate(
            flops=2 * half * stacked * (5 * KEYED + 3 * LATENT),
            bytes_accessed=16 * half * stacked,
            transcendentals=half * stacked,
        ),
    )(bounds_other, starts, slots, stats, q_cat, o_lat, w_key, other, keyed, expo, dprob)


def payload_kernel(mine_ref, got_ref, dq_ref, out_ref):
    piece = dq_ref.shape[2]
    slab = mine_ref.shape[1] - N_Z * piece
    own = slice(slab + piece, slab + N_Z * piece)
    for j in range(N_Y):
        out_ref[j, :slab, :] = (
            mine_ref[j, :slab, :].astype(F32) + got_ref[j, :slab, :].astype(F32)
        ).astype(BF16)
        parts = (mine_ref[j, own, :], got_ref[j, own, :], dq_ref[j, 0], dq_ref[j, 1])
        for i, part in enumerate(parts):
            out_ref[j, slab + i * piece : slab + (i + 1) * piece, :] = part


def near_payload(mine, got, dq):
    tall = mine.shape[1] + dq.shape[1] * dq.shape[2]
    vmem = pl.BlockSpec(memory_space=pltpu.VMEM)
    return pl.pallas_call(
        payload_kernel,
        out_shape=jax.ShapeDtypeStruct((N_Y, tall, LANES), BF16),
        in_specs=[vmem] * 3,
        out_specs=vmem,
        cost_estimate=pl.CostEstimate(
            flops=NEAR_FLOPS, bytes_accessed=6 * mine.size, transcendentals=0
        ),
    )(mine, got, dq)


def unpack_kernel(packed_ref, latent_ref, rope_ref):
    block = latent_ref.shape[0]
    for a in range(LATENT // LANES):
        latent_ref[:, a * LANES : (a + 1) * LANES] = packed_ref[a * block : (a + 1) * block, :]
    rope_ref[...] = packed_ref[LATENT // LANES * block :, :]


def unpack(packed):
    block = packed.shape[0] * LANES // KEYED
    vmem = pl.BlockSpec(memory_space=pltpu.VMEM)
    return pl.pallas_call(
        unpack_kernel,
        out_shape=[
            jax.ShapeDtypeStruct((block, LATENT), BF16),
            jax.ShapeDtypeStruct((ROPE, LANES), BF16),
        ],
        in_specs=[vmem],
        out_specs=[vmem] * 2,
        cost_estimate=pl.CostEstimate(
            flops=ORDER_FLOPS, bytes_accessed=4 * packed.size, transcendentals=0
        ),
    )(packed)


def shift(block, by):
    return lax.ppermute(block, "y", [(i, (i + by) % N_Y) for i in range(N_Y)])


def on_device(query, grad_out, latent, rope_key, w_key, w_value, offset):
    few = query.shape[0]
    n_sp = N_Y * N_Z * N_C
    block = latent.shape[0]
    folds = LATENT // LANES
    y, z, c = lax.axis_index("y"), lax.axis_index("z"), lax.axis_index("c")
    turned = rope_key.T.reshape(folds, ROPE // folds, block)
    pack = jnp.concatenate(
        [latent, jnp.transpose(turned, (1, 0, 2)).reshape(-1, LATENT)], axis=0
    )
    far = lax.ppermute(pack, "z", SWAP)
    qg = jnp.concatenate(
        [query.reshape(few, n_sp, -1), grad_out.reshape(few, n_sp, -1)], axis=2
    ).reshape(few, -1)
    qg, pack = lax.optimization_barrier((qg, pack))
    qg = lax.all_to_all(qg, ("y", "z", "c"), split_axis=1, concat_axis=0, tiled=True)
    both = jnp.stack([far, pack])
    mine = jnp.stack([both] + [shift(both, s) for s in range(1, N_Y)], axis=1)
    other = lax.ppermute(mine, "c", SWAP)

    steps = jnp.arange(N_Y, dtype=jnp.int32)

    def owner(y_of, z_of, c_of):
        return ((y_of * N_Z + z_of) * N_C + c_of).astype(jnp.int32)

    shifted = lax.rem(y - steps + N_Y, N_Y)
    owners = [
        jnp.concatenate([owner(shifted, z ^ dz, c_of) for dz in (1, 0)])
        for c_of in (c, c ^ 1)
    ]
    bounds_mine, bounds_other = (offset[0] - of * block for of in owners)
    starts = jnp.stack(
        [
            owner(steps[:, None], z ^ jnp.array([[1, 0]]), c ^ dc).reshape(-1)
            for dc in (1, 0)
        ]
    ).reshape(-1)
    d_other, d_mine, d_near_other, d_near_mine = attention(
        bounds_mine,
        bounds_other,
        starts * few,
        shifted.astype(jnp.int32),
        qg,
        w_key,
        w_value,
        mine,
        other,
    )
    slab = d_mine.shape[1]
    got = lax.ppermute(d_other, "c", SWAP)
    sent = (d_mine.astype(F32) + got.astype(F32)).astype(BF16)
    sent, d_near_other = lax.optimization_barrier((sent, d_near_other))
    near_got = lax.ppermute(d_near_other, "c", SWAP)
    piece = (d_near_mine.shape[1] - slab) // N_Z
    pieces = [d_near_mine[:, slab:], near_got[:, slab:]]
    dq_got = lax.ppermute(jnp.stack([p[:, :piece] for p in pieces], axis=1), "z", SWAP)
    slots = lax.all_to_all(sent, "y", split_axis=0, concat_axis=0, tiled=True)
    leaving = jnp.sum(slots.astype(F32), axis=0).astype(BF16)
    back = lax.ppermute(leaving, "z", SWAP)
    near = near_payload(d_near_mine, near_got, dq_got)
    near = lax.all_to_all(near, "y", split_axis=0, concat_axis=0, tiled=True)
    near_sum = jnp.sum(near[:, :slab].astype(F32), axis=0)
    back_latent, back_rope = unpack(back)
    near_latent = jnp.transpose(
        near_sum[: folds * block].reshape(folds, block, LANES), (1, 0, 2)
    ).reshape(block, LATENT)
    d_latent = (near_latent + back_latent.astype(F32)).astype(BF16)
    d_rope_key = (near_sum[folds * block :] + back_rope.astype(F32)).astype(BF16).T
    dq = near[:, slab:].reshape(N_Y, N_Z, N_C, -1, few, LANES)
    dq = jnp.where(z == 1, dq[:, ::-1], dq)
    dq = jnp.where(c == 1, dq[:, :, ::-1], dq)
    d_query = jnp.transpose(dq, (4, 0, 1, 2, 3, 5)).reshape(few, -1)
    return (d_query, d_latent, d_rope_key)


def solution(mesh):
    parts = mesh.devices.shape[0]
    split = Mesh(mesh.devices.reshape(parts, N_Y, N_Z, N_C), ("dp", "y", "z", "c"))
    rows = P(("dp", "y", "z", "c"), None)
    columns = P(None, ("y", "z", "c"))
    return jax.shard_map(
        on_device,
        mesh=split,
        in_specs=(rows, rows, rows, rows, columns, columns, P("dp")),
        out_specs=(rows, rows, rows),
        check_vma=False,
    )
```

```python
import math

import jax
import jax.numpy as jnp
from jax import lax
from jax.experimental import pallas as pl
from jax.experimental.pallas import tpu as pltpu
from jax.sharding import Mesh, PartitionSpec as P

NOPE = 128
ROPE = 64
VDIM = 128
LATENT = 512
LANES = 128
WIDTH = NOPE + ROPE
KEYED = LATENT + ROPE
N_Y, N_Z, N_C = 4, 2, 2
SWAP = [(0, 1), (1, 0)]
BF16 = jnp.bfloat16
F32 = jnp.float32
LOWEST = -1e29
HIDDEN = -1e30
EXPONENT = math.log2(math.e) * WIDTH ** (-0.5)
FIRST_FLOPS = 5_000_000_000
ORDER_FLOPS = 20_000_000_000
NEAR_FLOPS = 6_000_000_000


def dot(left, right, left_dim, right_dim):
    return lax.dot_general(
        left,
        right,
        (((left_dim,), (right_dim,)), ((), ())),
        preferred_element_type=F32,
    )


def unpack_keys(packed, keyed, base):
    block = packed.shape[1] * LATENT // KEYED
    folds = LATENT // LANES
    for j in range(N_Y):
        span = slice(base + j * block, base + (j + 1) * block)
        keyed[span, :LATENT] = packed[j, :block, :]
        rot = jnp.concatenate(
            [packed[j, block:, a * LANES : (a + 1) * LANES] for a in range(folds)], axis=0
        )
        keyed[span, LATENT:] = jnp.transpose(rot)


def owner(y, z, c):
    return (y * N_Z + z) * N_C + c


def behind(y, j):
    return lax.rem(y - j + N_Y, N_Y)


def forward_chunk(n, other, base, carry, where_ref, rel, keyed, q_cat, o_lat, expo, dprob):
    top, total, delta = carry
    block = rel.shape[0]
    span = slice(base, base + N_Y * block)
    scores = dot(keyed[span, :], q_cat[...], 1, 1)
    dp = dot(keyed[span, :LATENT], o_lat[...], 1, 1)
    dprob[span, :] = dp
    y, z, c, offset = (where_ref[i] for i in range(4))
    z_of = z if n == 1 else 1 - z
    c_of = 1 - c if other else c
    visible = [
        rel[...] <= offset - owner(behind(y, j), z_of, c_of) * block for j in range(N_Y)
    ]
    parts = [
        jnp.where(visible[j], scores[j * block : (j + 1) * block], HIDDEN)
        for j in range(N_Y)
    ]
    new_top = top
    for part in parts:
        new_top = jnp.maximum(new_top, jnp.max(part, axis=0, keepdims=True))
    keep = jnp.exp2((top - new_top) * EXPONENT)
    total = total * keep
    delta = delta * keep
    for j, part in enumerate(parts):
        e = jnp.exp2((part - new_top) * EXPONENT)
        expo[base + j * block : base + (j + 1) * block, :] = e
        total += jnp.sum(e, axis=0, keepdims=True)
        delta += jnp.sum(e * dp[j * block : (j + 1) * block], axis=0, keepdims=True)
    return new_top, total, delta


def set_relative(rel, count):
    rel[...] = lax.broadcasted_iota(jnp.int32, rel.shape, 0) - lax.rem(
        lax.broadcasted_iota(jnp.int32, rel.shape, 1), count
    )


def first_kernel(
    where_ref,
    qg_hbm,
    wk_hbm,
    wv_hbm,
    keys_hbm,
    q_cat_hbm,
    o_lat_hbm,
    keyed_hbm,
    expo_hbm,
    dprob_hbm,
    stats_ref,
    qg_ref,
    wk_ref,
    wv_ref,
    packed,
    keyed,
    q_cat,
    o_lat,
    rel,
    expo,
    dprob,
    in_sem,
    out_sem,
):
    count = qg_ref.shape[0]
    heads = wk_ref.shape[1] // NOPE
    stacked = heads * count
    chunk = N_Y * rel.shape[0]
    loads = [
        pltpu.make_async_copy(qg_hbm, qg_ref, in_sem.at[0]),
        pltpu.make_async_copy(wk_hbm, wk_ref, in_sem.at[1]),
        pltpu.make_async_copy(wv_hbm, wv_ref, in_sem.at[2]),
        pltpu.make_async_copy(keys_hbm, packed, in_sem.at[3]),
    ]
    for load in loads:
        load.start()
    set_relative(rel, count)
    for load in loads:
        load.wait()
    for h in range(heads):
        rows = slice(h * count, (h + 1) * count)
        cols = slice(h * NOPE, (h + 1) * NOPE)
        plain = qg_ref[:, h * WIDTH : h * WIDTH + NOPE]
        grad = qg_ref[:, heads * WIDTH + h * VDIM : heads * WIDTH + (h + 1) * VDIM]
        q_cat[rows, :LATENT] = dot(plain, wk_ref[:, cols], 1, 1).astype(BF16)
        q_cat[rows, LATENT:] = qg_ref[:, h * WIDTH + NOPE : (h + 1) * WIDTH]
        o_lat[rows, :] = dot(grad, wv_ref[:, cols], 1, 1).astype(BF16)
    carry = (
        jnp.full((1, stacked), LOWEST, F32),
        jnp.zeros((1, stacked), F32),
        jnp.zeros((1, stacked), F32),
    )
    stores = [
        pltpu.make_async_copy(q_cat, q_cat_hbm, out_sem.at[0]),
        pltpu.make_async_copy(o_lat, o_lat_hbm, out_sem.at[1]),
    ]
    for store in stores:
        store.start()
    for n in range(N_Z):
        unpack_keys(packed.at[n], keyed, n * chunk)
        carry = forward_chunk(
            n, False, n * chunk, carry, where_ref, rel, keyed, q_cat, o_lat, expo, dprob
        )
        span = pl.ds(n * chunk, chunk)
        for i, (mine, out) in enumerate(
            ((keyed, keyed_hbm), (expo, expo_hbm), (dprob, dprob_hbm))
        ):
            store = pltpu.make_async_copy(
                mine.at[span], out.at[span], out_sem.at[2 + 3 * n + i]
            )
            store.start()
            stores.append(store)
        stats_ref[n : n + 1, :] = carry[0]
    stats_ref[N_Z : N_Z + 1, :] = carry[1]
    stats_ref[N_Z + 1 : N_Z + 2, :] = carry[2]
    for store in stores:
        store.wait()


def second_kernel(
    where_ref,
    stats_ref,
    q_cat_hbm,
    o_lat_hbm,
    wk_hbm,
    keys_hbm,
    keyed_hbm,
    expo_hbm,
    dprob_hbm,
    d_far_other_hbm,
    d_far_mine_hbm,
    d_near_other_hbm,
    d_near_mine_hbm,
    wk_ref,
    packed,
    keyed,
    d_near,
    d_far,
    dq_ref,
    q_cat,
    o_lat,
    rel,
    expo,
    dprob,
    in_sem,
    out_sem,
):
    scale = WIDTH ** (-0.5)
    y, z, c = (where_ref[i] for i in range(3))
    heads = wk_ref.shape[1] // NOPE
    stacked = q_cat.shape[0]
    count = stacked // heads
    block = rel.shape[0]
    chunk = N_Y * block
    half = N_Z * chunk
    folds = LATENT // LANES
    slab = folds * block + ROPE
    late = pl.ds(half, half)
    loads = [
        pltpu.make_async_copy(keys_hbm, packed, in_sem.at[0]),
        pltpu.make_async_copy(q_cat_hbm, q_cat, in_sem.at[1]),
        pltpu.make_async_copy(o_lat_hbm, o_lat, in_sem.at[2]),
        pltpu.make_async_copy(keyed_hbm, keyed.at[late], in_sem.at[3]),
        pltpu.make_async_copy(expo_hbm, expo.at[late], in_sem.at[4]),
        pltpu.make_async_copy(dprob_hbm, dprob.at[late], in_sem.at[5]),
        pltpu.make_async_copy(wk_hbm, wk_ref, in_sem.at[6]),
    ]
    for load in loads:
        load.start()
    set_relative(rel, count)
    for load in loads[:3]:
        load.wait()
    carry = (
        stats_ref[N_Z - 1 : N_Z, :],
        stats_ref[N_Z : N_Z + 1, :],
        stats_ref[N_Z + 1 : N_Z + 2, :],
    )
    tops = []
    for n in range(N_Z):
        unpack_keys(packed.at[n], keyed, n * chunk)
        carry = forward_chunk(
            n, True, n * chunk, carry, where_ref, rel, keyed, q_cat, o_lat, expo, dprob
        )
        tops.append(carry[0])
    tops += [stats_ref[n : n + 1, :] for n in range(N_Z)]
    for load in loads[3:]:
        load.wait()
    top, total, delta = carry
    inverse = 1.0 / total
    delta = delta * inverse
    dq_lat = jnp.zeros((stacked, KEYED), F32)
    stores = []
    for m in (0, 2, 1, 3):
        z_slot, c_slot = m % N_Z, m // N_Z
        span = slice(m * chunk, (m + 1) * chunk)
        probs = expo[span, :] * (jnp.exp2((tops[m] - top) * EXPONENT) * inverse)
        dscore = (probs * (dprob[span, :] - delta) * scale).astype(BF16)
        probs_low = probs.astype(BF16)
        d_key = dot(dscore, q_cat[...], 1, 0)
        d_lat = (d_key[:, :LATENT] + dot(probs_low, o_lat[...], 1, 0)).astype(BF16)
        d_rot = d_key[:, LATENT:].astype(BF16)
        for j in range(N_Y):
            rows = slice(j * block, (j + 1) * block)
            place = (d_far, d_near)[z_slot].at[c_slot, behind(y, j)]
            for a in range(folds):
                place[a * block : (a + 1) * block, :] = d_lat[
                    rows, a * LANES : (a + 1) * LANES
                ]
            place[folds * block : slab, :] = jnp.transpose(d_rot[rows])
        if z_slot == 0:
            store = pltpu.make_async_copy(
                d_far.at[c_slot],
                (d_far_other_hbm, d_far_mine_hbm)[c_slot],
                out_sem.at[c_slot],
            )
            store.start()
            stores.append(store)
        dq_lat += dot(dscore, keyed[span, :], 0, 0)
    dq_low = dq_lat.astype(BF16)
    for h in range(heads):
        rows = slice(h * count, (h + 1) * count)
        cols = slice(h * NOPE, (h + 1) * NOPE)
        dq_ref[:, h * WIDTH : h * WIDTH + NOPE] = dot(
            dq_low[rows, :LATENT], wk_ref[:, cols], 1, 0
        )
        dq_ref[:, h * WIDTH + NOPE : (h + 1) * WIDTH] = dq_lat[rows, LATENT:]
    few = count // (N_Y * N_Z * N_C)
    for n in range(N_C):
        for j in range(N_Y):
            pieces = []
            for dz in range(N_Z):
                z_of = z if dz == 1 else 1 - z
                c_of = c if n == 1 else 1 - c
                start = pl.multiple_of(owner(j, z_of, c_of) * few, few)
                for a in range(heads * WIDTH // LANES):
                    pieces.append(dq_ref[pl.ds(start, few), a * LANES : (a + 1) * LANES])
            d_near[n, j, slab:, :] = jnp.concatenate(pieces, axis=0).astype(BF16)
        store = pltpu.make_async_copy(
            d_near.at[n], (d_near_other_hbm, d_near_mine_hbm)[n], out_sem.at[N_C + n]
        )
        store.start()
        stores.append(store)
    for store in stores:
        store.wait()


def attention(where, qg, w_key, w_value, mine, other):
    count = qg.shape[0]
    heads = w_key.shape[1] // NOPE
    stacked = heads * count
    tall = mine.shape[2]
    block = tall * LATENT // KEYED
    half = N_Z * N_Y * block
    slab = block * KEYED // LANES
    extra = N_Z * (count // (N_Y * N_Z * N_C)) * heads * WIDTH // LANES
    near_slab = slab + extra
    hbm = pl.BlockSpec(memory_space=pl.ANY)
    smem = pl.BlockSpec(memory_space=pltpu.SMEM)
    vmem = pl.BlockSpec(memory_space=pltpu.VMEM)
    middle = [
        jax.ShapeDtypeStruct((stacked, KEYED), BF16),
        jax.ShapeDtypeStruct((stacked, LATENT), BF16),
        jax.ShapeDtypeStruct((half, KEYED), BF16),
        jax.ShapeDtypeStruct((half, stacked), F32),
        jax.ShapeDtypeStruct((half, stacked), F32),
        jax.ShapeDtypeStruct((8, stacked), F32),
    ]
    q_cat, o_lat, keyed, expo, dprob, stats = pl.pallas_call(
        first_kernel,
        out_shape=middle,
        in_specs=[smem] + [hbm] * 4,
        out_specs=[hbm] * 5 + [vmem],
        scratch_shapes=[
            pltpu.VMEM(qg.shape, BF16),
            pltpu.VMEM(w_key.shape, BF16),
            pltpu.VMEM(w_value.shape, BF16),
            pltpu.VMEM(mine.shape, BF16),
            pltpu.VMEM((half, KEYED), BF16),
            pltpu.VMEM((stacked, KEYED), BF16),
            pltpu.VMEM((stacked, LATENT), BF16),
            pltpu.VMEM((block, stacked), jnp.int32),
            pltpu.VMEM((half, stacked), F32),
            pltpu.VMEM((half, stacked), F32),
            pltpu.SemaphoreType.DMA((4,)),
            pltpu.SemaphoreType.DMA((2 + 3 * N_Z,)),
        ],
        compiler_params=pltpu.CompilerParams(vmem_limit_bytes=56 * 2**20),
        cost_estimate=pl.CostEstimate(
            flops=FIRST_FLOPS, bytes_accessed=12 * half * stacked, transcendentals=half * stacked
        ),
    )(where, qg, w_key, w_value, mine)
    return pl.pallas_call(
        second_kernel,
        out_shape=[jax.ShapeDtypeStruct((N_Y, slab, LANES), BF16)] * N_C
        + [jax.ShapeDtypeStruct((N_Y, near_slab, LANES), BF16)] * N_C,
        in_specs=[smem, vmem] + [hbm] * 7,
        out_specs=[hbm] * 4,
        scratch_shapes=[
            pltpu.VMEM(w_key.shape, BF16),
            pltpu.VMEM(other.shape, BF16),
            pltpu.VMEM((2 * half, KEYED), BF16),
            pltpu.VMEM((N_C, N_Y, near_slab, LANES), BF16),
            pltpu.VMEM((N_C, N_Y, slab, LANES), BF16),
            pltpu.VMEM((count, heads * WIDTH), F32),
            pltpu.VMEM((stacked, KEYED), BF16),
            pltpu.VMEM((stacked, LATENT), BF16),
            pltpu.VMEM((block, stacked), jnp.int32),
            pltpu.VMEM((2 * half, stacked), F32),
            pltpu.VMEM((2 * half, stacked), F32),
            pltpu.SemaphoreType.DMA((7,)),
            pltpu.SemaphoreType.DMA((2 * N_C,)),
        ],
        compiler_params=pltpu.CompilerParams(vmem_limit_bytes=56 * 2**20),
        cost_estimate=pl.CostEstimate(
            flops=2 * half * stacked * (5 * KEYED + 3 * LATENT),
            bytes_accessed=16 * half * stacked,
            transcendentals=half * stacked,
        ),
    )(where, stats, q_cat, o_lat, w_key, other, keyed, expo, dprob)


def payload_kernel(mine_ref, got_ref, dq_ref, out_ref):
    piece = dq_ref.shape[2]
    slab = mine_ref.shape[1] - N_Z * piece
    own = slice(slab + piece, slab + N_Z * piece)
    for j in range(N_Y):
        out_ref[j, :slab, :] = (
            mine_ref[j, :slab, :].astype(F32) + got_ref[j, :slab, :].astype(F32)
        ).astype(BF16)
        parts = (mine_ref[j, own, :], got_ref[j, own, :], dq_ref[j, 0], dq_ref[j, 1])
        for i, part in enumerate(parts):
            out_ref[j, slab + i * piece : slab + (i + 1) * piece, :] = part


def near_payload(mine, got, dq):
    tall = mine.shape[1] + dq.shape[1] * dq.shape[2]
    vmem = pl.BlockSpec(memory_space=pltpu.VMEM)
    return pl.pallas_call(
        payload_kernel,
        out_shape=jax.ShapeDtypeStruct((N_Y, tall, LANES), BF16),
        in_specs=[vmem] * 3,
        out_specs=vmem,
        cost_estimate=pl.CostEstimate(
            flops=NEAR_FLOPS, bytes_accessed=6 * mine.size, transcendentals=0
        ),
    )(mine, got, dq)


def unpack_kernel(packed_ref, latent_ref, rope_ref):
    block = latent_ref.shape[0]
    for a in range(LATENT // LANES):
        latent_ref[:, a * LANES : (a + 1) * LANES] = packed_ref[a * block : (a + 1) * block, :]
    rope_ref[...] = packed_ref[LATENT // LANES * block :, :]


def unpack(packed):
    block = packed.shape[0] * LANES // KEYED
    vmem = pl.BlockSpec(memory_space=pltpu.VMEM)
    return pl.pallas_call(
        unpack_kernel,
        out_shape=[
            jax.ShapeDtypeStruct((block, LATENT), BF16),
            jax.ShapeDtypeStruct((ROPE, LANES), BF16),
        ],
        in_specs=[vmem],
        out_specs=[vmem] * 2,
        cost_estimate=pl.CostEstimate(
            flops=ORDER_FLOPS, bytes_accessed=4 * packed.size, transcendentals=0
        ),
    )(packed)


def shift(block, by):
    return lax.ppermute(block, "y", [(i, (i + by) % N_Y) for i in range(N_Y)])


def on_device(query, grad_out, latent, rope_key, w_key, w_value, offset):
    few = query.shape[0]
    n_sp = N_Y * N_Z * N_C
    block = latent.shape[0]
    folds = LATENT // LANES
    y, z, c = lax.axis_index("y"), lax.axis_index("z"), lax.axis_index("c")
    turned = rope_key.T.reshape(folds, ROPE // folds, block)
    pack = jnp.concatenate(
        [latent, jnp.transpose(turned, (1, 0, 2)).reshape(-1, LATENT)], axis=0
    )
    far = lax.ppermute(pack, "z", SWAP)
    qg = jnp.concatenate(
        [query.reshape(few, n_sp, -1), grad_out.reshape(few, n_sp, -1)], axis=2
    ).reshape(few, -1)
    qg, pack = lax.optimization_barrier((qg, pack))
    qg = lax.all_to_all(qg, ("y", "z", "c"), split_axis=1, concat_axis=0, tiled=True)
    both = jnp.stack([far, pack])
    mine = jnp.stack([both] + [shift(both, s) for s in range(1, N_Y)], axis=1)
    other = lax.ppermute(mine, "c", SWAP)

    where = jnp.stack([y, z, c, offset[0]]).astype(jnp.int32)
    d_other, d_mine, d_near_other, d_near_mine = attention(
        where,
        qg,
        w_key,
        w_value,
        mine,
        other,
    )
    slab = d_mine.shape[1]
    got = lax.ppermute(d_other, "c", SWAP)
    sent = (d_mine.astype(F32) + got.astype(F32)).astype(BF16)
    sent, d_near_other = lax.optimization_barrier((sent, d_near_other))
    near_got = lax.ppermute(d_near_other, "c", SWAP)
    piece = (d_near_mine.shape[1] - slab) // N_Z
    pieces = [d_near_mine[:, slab:], near_got[:, slab:]]
    dq_got = lax.ppermute(jnp.stack([p[:, :piece] for p in pieces], axis=1), "z", SWAP)
    slots = lax.all_to_all(sent, "y", split_axis=0, concat_axis=0, tiled=True)
    leaving = jnp.sum(slots.astype(F32), axis=0).astype(BF16)
    back = lax.ppermute(leaving, "z", SWAP)
    near = near_payload(d_near_mine, near_got, dq_got)
    near = lax.all_to_all(near, "y", split_axis=0, concat_axis=0, tiled=True)
    near_sum = jnp.sum(near[:, :slab].astype(F32), axis=0)
    back_latent, back_rope = unpack(back)
    near_latent = jnp.transpose(
        near_sum[: folds * block].reshape(folds, block, LANES), (1, 0, 2)
    ).reshape(block, LATENT)
    d_latent = (near_latent + back_latent.astype(F32)).astype(BF16)
    d_rope_key = (near_sum[folds * block :] + back_rope.astype(F32)).astype(BF16).T
    dq = near[:, slab:].reshape(N_Y, N_Z, N_C, -1, few, LANES)
    dq = jnp.where(z == 1, dq[:, ::-1], dq)
    dq = jnp.where(c == 1, dq[:, :, ::-1], dq)
    d_query = jnp.transpose(dq, (4, 0, 1, 2, 3, 5)).reshape(few, -1)
    return (d_query, d_latent, d_rope_key)


def solution(mesh):
    parts = mesh.devices.shape[0]
    split = Mesh(mesh.devices.reshape(parts, N_Y, N_Z, N_C), ("dp", "y", "z", "c"))
    rows = P(("dp", "y", "z", "c"), None)
    columns = P(None, ("y", "z", "c"))
    return jax.shard_map(
        on_device,
        mesh=split,
        in_specs=(rows, rows, rows, rows, columns, columns, P("dp")),
        out_specs=(rows, rows, rows),
        check_vma=False,
    )
```
